128 devices in a mesh: ta: 4 (over z), ha: 8 (over x, y_lo), wa: 4 (over y_hi, core).
Axes of the slice: x: 4, y: 4 (y_hi: 2, y_lo: 2; y = y_hi * 2 + y_lo), z: 4, core: 2. Of those that a mesh axis runs over, the one named last changes fastest.
Arguments:
- queries: bfloat16 [8, 8, 4, 192, 1536], P('ta', 'ha', 'wa'), may hold values from -100 to 100
- keys: bfloat16 [8, 8, 4, 192, 1536], P('ta', 'ha', 'wa'), may hold values from -6 to 6
- values: bfloat16 [8, 8, 4, 192, 1536], P('ta', 'ha', 'wa'), may hold values from -6 to 6
- valid_counts: int32 [8, 8, 4], replicated, may hold values from 2 to 192, as said below
- head_window: int32 [12, 3], replicated, may hold values from 0 to 1
Outputs:
- attended: bfloat16 [8, 8, 4, 192, 1536], P('ta', 'ha', 'wa')
The draws below stay inside these ranges and needn't reach their ends.
Inputs may be any that keep to these rules, and one draw needn't show every extreme that they name: `valid_counts`: every tile that is not on the last layer of tiles along time, height or width holds 192 live tokens; the last tile along all three holds 2.
All inputs are finite; a program needn't handle non-finite values.
Results may differ from the reference program's by a relative error of at most 0.0049.
Values may be sent and summed in bfloat16 or wider, within the bound.
No kernel may reach another device: no remote copies, remote signals or barrier semaphores. Data moves between devices by JAX's collectives and lax.ppermute only.
A program may use at most 256 MiB of HBM per device.

```python
import jax
import jax.numpy as jnp
from jax import lax

HEADS = 12
HEAD_DIM = 128
TILE_TOK = 192
FEAT = 1536
NT = 8
NH = 8
NW = 4


def shared_keys(key):
    base = jax.random.normal(key, (NT, NH, NW, TILE_TOK, HEADS * HEAD_DIM), jnp.float32)
    return jnp.clip(base, -5.0, 5.0)


def draw_keys(key, part):
    base = shared_keys(key)
    result = base
    return result.astype(jnp.bfloat16)


def draw_queries(key, part):
    base = shared_keys(key)
    key = jax.random.fold_in(key, 5)
    own = jnp.clip(jax.random.normal(key, base.shape, jnp.float32), -5.0, 5.0)
    return own.astype(jnp.bfloat16)


def draw_valid_counts(key, part):
    key = jax.random.fold_in(key, 9)
    t_pos = jnp.arange(NT, dtype=jnp.int32)[:, None, None]
    h_pos = jnp.arange(NH, dtype=jnp.int32)[None, :, None]
    w_pos = jnp.arange(NW, dtype=jnp.int32)[None, None, :]
    border = (t_pos == NT - 1) | (h_pos == NH - 1) | (w_pos == NW - 1)
    partial_value = jax.random.randint(key, (NT, NH, NW), 2, TILE_TOK + 1)
    counts = jnp.where(border, partial_value, TILE_TOK)
    return counts.at[NT - 1, NH - 1, NW - 1].set(2).astype(jnp.int32)


def with_ends(drawn, key, least, top_value):
    shape = drawn.shape
    place = [jax.random.randint(jax.random.fold_in(key, axis), (), 0, shape[axis]) for axis in range(len(shape))]
    drawn = drawn.at[tuple(place)].set(least)
    longest = shape.index(max(shape))
    place[longest] = (place[longest] + 1) % shape[longest]
    return drawn.at[tuple(place)].set(top_value)


def block_levels(rng, extent, split, low, top_value):
    def one(position, blocks):
        draws = jax.random.uniform(jax.random.fold_in(jax.random.fold_in(rng, 6), position), (blocks,), jnp.float32, low / len(split), top_value / len(split))
        return jnp.repeat(jnp.exp(draws), extent[position] // blocks).reshape((-1,) + (1,) * (len(extent) - position - 1))

    loudness = one(*split[0])
    for cut in split[1:]:
        loudness = loudness * one(*cut)
    return loudness


def centred(stream_key, extent, deviation, limit, pieces=(), held_as=jnp.bfloat16):
    entries = deviation * jax.random.normal(stream_key, extent, jnp.float32)
    if pieces:
        entries = entries * block_levels(stream_key, extent, pieces, -0.22, 0.18)
    return jnp.clip(entries, -limit, limit).astype(held_as)


def setup_inputs(seed: int = 0) -> dict:
    key_list = jax.random.split(jax.random.key(seed), 6)
    queries = draw_queries(jax.random.fold_in(key_list[5], 71), 0)
    keys = draw_keys(jax.random.fold_in(key_list[5], 71), 0)
    values = centred(key_list[2], (NT, NH, NW, TILE_TOK, FEAT), 1.0, 6.0, ((0, 4), (1, 8), (2, 4)))
    valid_counts = draw_valid_counts(jax.random.fold_in(key_list[5], 71), 0)
    head_window = with_ends(jax.random.randint(key_list[4], (HEADS, 3), 0, 2), jax.random.fold_in(key_list[4], 1), 0, 1).astype(jnp.int32)
    return dict(queries=queries, keys=keys, values=values, valid_counts=valid_counts, head_window=head_window)


def attend(q_tile, near_keys, near_values, near_counts, head_window):
    tok = q_tile.shape[0]
    offsets = jnp.arange(27, dtype=jnp.int32)
    off_t = offsets // 9 - 1
    off_h = (offsets // 3) % 3 - 1
    off_w = offsets % 3 - 1
    token_pos = jnp.arange(tok, dtype=jnp.int32)
    key_live = (token_pos[None, :] < near_counts[:, None]).reshape(-1)
    query_live = token_pos < near_counts[13]
    scale = HEAD_DIM ** -0.5

    def one_head(head):
        reach = head_window[head]
        allowed = (jnp.abs(off_t) <= reach[0]) & (jnp.abs(off_h) <= reach[1]) & (jnp.abs(off_w) <= reach[2])
        live = key_live & jnp.repeat(allowed, tok, total_repeat_length=27 * tok)
        start = head * HEAD_DIM
        q_head = lax.dynamic_slice_in_dim(q_tile, start, HEAD_DIM, 1)
        k_head = lax.dynamic_slice_in_dim(near_keys, start, HEAD_DIM, 1)
        v_head = lax.dynamic_slice_in_dim(near_values, start, HEAD_DIM, 1)
        scores = lax.dot_general(q_head, k_head, (((1,), (1,)), ((), ())), preferred_element_type=jnp.float32) * scale
        scores = jnp.where(live[None, :], scores, -1e30)
        top = jnp.max(scores, axis=1, keepdims=True)
        weights = jnp.where(live[None, :], jnp.exp(scores - top), 0.0)
        probs = (weights / jnp.sum(weights, axis=1, keepdims=True)).astype(jnp.bfloat16)
        return jnp.dot(probs, v_head, preferred_element_type=jnp.float32)

    heads_out = lax.map(one_head, jnp.arange(HEADS, dtype=jnp.int32))
    heads_out = jnp.where(query_live[None, :, None], heads_out, 0.0)
    return heads_out.transpose(1, 0, 2).reshape(tok, HEADS * HEAD_DIM).astype(jnp.bfloat16)


def reference(queries, keys, values, valid_counts, head_window):
    grid_pad = ((1, 1), (1, 1), (1, 1), (0, 0), (0, 0))
    key_pad = jnp.pad(keys, grid_pad)
    value_pad = jnp.pad(values, grid_pad)
    count_pad = jnp.pad(valid_counts, 1)
    zero = jnp.zeros((), jnp.int32)
    feat = HEADS * HEAD_DIM

    def one_tile(index):
        t_pos = index // (NH * NW)
        h_pos = (index // NW) % NH
        w_pos = index % NW
        q_tile = lax.dynamic_slice(queries, (t_pos, h_pos, w_pos, zero, zero), (1, 1, 1, TILE_TOK, feat)).reshape(TILE_TOK, feat)
        near_keys = lax.dynamic_slice(key_pad, (t_pos, h_pos, w_pos, zero, zero), (3, 3, 3, TILE_TOK, feat)).reshape(27 * TILE_TOK, feat)
        near_values = lax.dynamic_slice(value_pad, (t_pos, h_pos, w_pos, zero, zero), (3, 3, 3, TILE_TOK, feat)).reshape(27 * TILE_TOK, feat)
        near_counts = lax.dynamic_slice(count_pad, (t_pos, h_pos, w_pos), (3, 3, 3)).reshape(27)
        return attend(q_tile, near_keys, near_values, near_counts, head_window)

    tiles = lax.map(one_tile, jnp.arange(NT * NH * NW, dtype=jnp.int32))
    return tiles.reshape(NT, NH, NW, TILE_TOK, feat)
```

```python
import functools

import jax
import jax.numpy as jnp
from jax import lax
from jax.experimental import pallas as pl
from jax.experimental.pallas import tpu as pltpu
from jax.sharding import PartitionSpec as P

HEADS = 12
DIM = 128
TOK = 192
NT, NH, NW = 8, 8, 4
RING = 4
SLOTS = HEADS // RING
CHUNK = 4
LOG2E = 1.4426950408889634
ITEMS = 32
SCALE = DIM**-0.5 * LOG2E
PLANE = ("ha", "wa")
ANY = pl.BlockSpec(memory_space=pl.ANY)
SMEM = pl.BlockSpec(memory_space=pltpu.SMEM)
VMEM = pl.BlockSpec(memory_space=pltpu.VMEM)


def plane_index(x, y, core):
    return (x * 2 + y % 2) * 4 + (y // 2) * 2 + core


PLANE_POS = [(x, y, core) for x in range(4) for y in range(4) for core in range(2)]


def ring_swap(block, mask):
    perm = [(plane_index(x, y, c), plane_index(x, y ^ mask, c)) for x, y, c in PLANE_POS]
    return lax.ppermute(block, PLANE, perm)


def core_swap(block):
    perm = [(plane_index(x, y, c), plane_index(x, y, 1 - c)) for x, y, c in PLANE_POS]
    return lax.ppermute(block, PLANE, perm)


def row_step(block, own):
    perm = []
    for x, y, c in PLANE_POS:
        target = x + 1 if (y % 2 == 1) == own else x - 1
        if 0 <= target < 4:
            perm.append((plane_index(x, y, c), plane_index(target, y, c)))
    return lax.ppermute(block, PLANE, perm)


def depth_step(block, step):
    return lax.ppermute(block, "ta", [(i, i + step) for i in range(4) if 0 <= i + step < 4])


def place():
    plane_h = lax.axis_index("ha")
    plane_w = lax.axis_index("wa")
    return lax.axis_index("ta"), plane_h // 2, plane_h % 2, plane_w // 2, plane_w % 2


def rank_heads(window, order):
    keys = []
    for head in range(HEADS):
        reach = window[head, 0] * 4 + window[head, 1] * 2 + window[head, 2]
        keys.append((7 - reach) * 16 + head)
    for head in range(HEADS):
        rank = jnp.int32(0)
        for other in range(HEADS):
            if other != head:
                rank += (keys[other] < keys[head]).astype(jnp.int32)
        order[rank] = head


def pack_kernel(slots, parts, window, *rest):
    sources = rest[:parts]
    outs = rest[parts : parts + RING]
    order, sem = rest[parts + RING :]
    rank_heads(window, order)
    _, _, y_lo, y_hi, _ = place()
    ring = y_hi * 2 + y_lo
    copies = []
    for n, slot in enumerate(slots):
        for mask in range(RING):
            head = order[slot * RING + (ring ^ mask)]
            cols = pl.ds(pl.multiple_of(head * DIM, DIM), DIM)
            for part in range(parts):
                for t in range(2):
                    copies.append(
                        pltpu.make_async_copy(
                            sources[part].at[t, 0, 0, :, cols], outs[mask].at[n, t, part], sem
                        )
                    )
    for copy in copies:
        copy.start()
    for copy in copies:
        copy.wait()


def pack(slots, head_window, *sources):
    shape = jax.ShapeDtypeStruct((len(slots), 2, len(sources), TOK, DIM), jnp.bfloat16)
    return pl.pallas_call(
        functools.partial(pack_kernel, slots, len(sources)),
        out_shape=[shape] * RING,
        in_specs=[SMEM] + [VMEM] * len(sources),
        out_specs=[ANY] * RING,
        scratch_shapes=[pltpu.SMEM((HEADS,), jnp.int32), pltpu.SemaphoreType.DMA],
        compiler_params=pltpu.CompilerParams(vmem_limit_bytes=16 * 1024 * 1024),
        cost_estimate=pl.CostEstimate(flops=0, bytes_accessed=7_000_000, transcendentals=0),
    )(head_window, *sources)


def unpack_kernel(window, *rest):
    parts = rest[:RING]
    out, order, sem = rest[RING:]
    rank_heads(window, order)
    _, _, y_lo, y_hi, _ = place()
    ring = y_hi * 2 + y_lo
    copies = []
    for slot in range(SLOTS):
        for mask in range(RING):
            head = order[slot * RING + (ring ^ mask)]
            cols = pl.ds(pl.multiple_of(head * DIM, DIM), DIM)
            for t in range(2):
                copies.append(
                    pltpu.make_async_copy(
                        parts[mask].at[slot, t], out.at[t, 0, 0, :, cols], sem
                    )
                )
    for copy in copies:
        copy.start()
    for copy in copies:
        copy.wait()


def unpack(head_window, parts):
    return pl.pallas_call(
        unpack_kernel,
        out_shape=jax.ShapeDtypeStruct((2, 1, 1, TOK, HEADS * DIM), jnp.bfloat16),
        in_specs=[SMEM] + [ANY] * RING,
        out_specs=VMEM,
        scratch_shapes=[pltpu.SMEM((HEADS,), jnp.int32), pltpu.SemaphoreType.DMA],
        compiler_params=pltpu.CompilerParams(vmem_limit_bytes=8 * 1024 * 1024),
        cost_estimate=pl.CostEstimate(flops=0, bytes_accessed=2_400_000, transcendentals=0),
    )(head_window, *parts)


def list_tiles(counts, items, lives, reach, glob, t, y_lo, y_hi, core, w):
    glob_t, glob_h = glob
    h = glob_h % 2

    def axis(position, extent, reach_here, code):
        out = []
        for step in (0, -1, 1):
            spot = position + step
            inside = (spot >= 0) & (spot < extent) & (abs(step) <= reach_here)
            out.append((inside.astype(jnp.int32), jnp.clip(spot, 0, extent - 1), code(step)))
        return out

    def code_t(step):
        here = t + step
        return {0: 0, 1: 8, -1: 16, 2: 24}[here]

    def code_h(step):
        here = h + step
        row = jnp.where(here < 0, 1, jnp.where(here > 1, 0, here))
        halo = ((here < 0) | (here > 1)).astype(jnp.int32)
        return halo * 4 + (row ^ y_lo) * 2

    def code_w(step):
        here = w + step
        here = jnp.clip(here, 0, NW - 1)
        return (here % 2 != core).astype(jnp.int32) * ITEMS + ((here // 2) ^ y_hi)

    over_t = axis(glob_t, NT, reach[0], code_t)
    over_h = axis(glob_h, NH, reach[1], code_h)
    over_w = axis(w, NW, reach[2], code_w)
    total = jnp.int32(0)
    for in_t, at_t, item_t in over_t:
        for in_h, at_h, item_h in over_h:
            for in_w, at_w, item_w in over_w:
                items[t, total] = item_t + item_h + item_w
                lives[t, total] = counts[at_t, at_h, at_w]
                total += in_t * in_h * in_w
    return total


def attend_kernel(slots, window, counts, *rest):
    kvs = rest[0]
    q_in = rest[1 : 1 + RING]
    outs = rest[1 + RING : 1 + 2 * RING]
    order, items, lives = rest[1 + 2 * RING :]
    rank_heads(window, order)
    z, x, y_lo, y_hi, core = place()
    for n, slot in enumerate(slots):
        head = order[slot * RING + y_hi * 2 + y_lo]
        reach = [window[head, axis] for axis in range(3)]
        for mask in range(RING):
            h = (mask % 2) ^ y_lo
            w = 2 * ((mask // 2) ^ y_hi) + core
            glob_h = 2 * x + h
            totals, owns = [], []
            for t in range(2):
                owns.append(counts[2 * z + t, glob_h, w])
                totals.append(
                    list_tiles(
                        counts, items, lives, reach, (2 * z + t, glob_h), t, y_lo, y_hi, core, w
                    )
                )
            chunks = (jnp.maximum(totals[0], totals[1]) + CHUNK - 1) // CHUNK
            for t in range(2):

                def fill(spot, carry):
                    items[t, spot] = items[t, 0]
                    lives[t, spot] = 0
                    return carry

                lax.fori_loop(totals[t], chunks * CHUNK, fill, 0)

            query = [q_in[mask][n, t, 0] for t in range(2)]

            def one_chunk(chunk, state):
                first = chunk * CHUNK
                after = []
                for t in range(2):
                    top, acc = state[2 * t : 2 * t + 2]
                    spots = [items[t, first + u] for u in range(CHUNK)]
                    k_all = jnp.concatenate([kvs[n, spot, 0] for spot in spots], axis=0)
                    v_all = jnp.concatenate([kvs[n, spot, 1] for spot in spots], axis=0)
                    ones = jnp.ones((CHUNK * TOK, DIM), jnp.bfloat16)
                    v_all = jnp.concatenate([v_all, ones], axis=1)
                    scores = lax.dot_general(
                        query[t], k_all, (((1,), (1,)), ((), ())),
                        preferred_element_type=jnp.float32,
                    )
                    column = lax.broadcasted_iota(jnp.int32, (1, CHUNK * TOK), 1)
                    bias = jnp.full((1, CHUNK * TOK), -1e30, jnp.float32)
                    for u in range(CHUNK):
                        edge = u * TOK
                        live = (column >= edge) & (column < edge + lives[t, first + u])
                        bias = jnp.where(live, 0.0, bias)
                    scores = scores * SCALE + bias
                    new_top = jnp.maximum(top, jnp.max(scores, axis=1, keepdims=True))
                    weights = jnp.exp2(scores - new_top).astype(jnp.bfloat16)
                    gain = jnp.dot(weights, v_all, preferred_element_type=jnp.float32)
                    after += [new_top, acc * jnp.exp2(top - new_top) + gain]
                return tuple(after)

            start = (
                jnp.full((TOK, 1), -3e30, jnp.float32),
                jnp.zeros((TOK, 2 * DIM), jnp.float32),
            )
            state = lax.fori_loop(0, chunks, one_chunk, start * 2)
            for t in range(2):
                acc = state[2 * t + 1]
                result = acc[:, :DIM] / acc[:, DIM:]
                row = lax.broadcasted_iota(jnp.int32, (TOK, DIM), 0)
                outs[mask][n, t] = jnp.where(row < owns[t], result, 0.0).astype(jnp.bfloat16)


def attend(slots, head_window, valid_counts, kvs, q_parts):
    shape = jax.ShapeDtypeStruct((len(slots), 2, TOK, DIM), jnp.bfloat16)
    return pl.pallas_call(
        functools.partial(attend_kernel, slots),
        out_shape=[shape] * RING,
        in_specs=[SMEM, SMEM] + [VMEM] * (1 + RING),
        out_specs=[VMEM] * RING,
        scratch_shapes=[
            pltpu.SMEM((HEADS,), jnp.int32),
            pltpu.SMEM((2, 27 + CHUNK), jnp.int32),
            pltpu.SMEM((2, 27 + CHUNK), jnp.int32),
        ],
        compiler_params=pltpu.CompilerParams(vmem_limit_bytes=32 * 1024 * 1024),
        cost_estimate=pl.CostEstimate(
            flops=len(slots) * 8_000_000_000,
            bytes_accessed=len(slots) * 6_500_000,
            transcendentals=len(slots) * 5_000_000,
        ),
    )(head_window, valid_counts, kvs, *q_parts)


def spread(parts):
    return [parts[0]] + [ring_swap(parts[mask], mask) for mask in range(1, RING)]


def with_rows(a):
    x_own = row_step(jnp.stack([a[0], a[2]], axis=2), True)
    x_other = row_step(jnp.stack([a[1], a[3]], axis=2), False)
    inner = jnp.stack([a[0], a[2], a[1], a[3]], axis=2)
    return jnp.concatenate([inner, x_own, x_other], axis=2)


def on_device(queries, keys, values, valid_counts, head_window):
    light = (1, 2)
    a_parts = pack((0,), head_window, keys, values, queries)
    b_parts = pack(light, head_window, keys, values)
    c_parts = pack(light, head_window, queries)
    a_all = spread(a_parts)
    b = spread(b_parts)
    c = spread(c_parts)

    near_a = with_rows([block[:, :, :2] for block in a_all])
    low_a = depth_step(near_a[:, 1], 1)
    high_a = depth_step(near_a[:, 0], -1)
    mine_a = [near_a.reshape(1, 16, 2, TOK, DIM), low_a, high_a]
    kv_a = jnp.concatenate(mine_a + [core_swap(block) for block in mine_a], axis=1)
    out_a = attend((0,), head_window, valid_counts, kv_a, [block[:, :, 2:] for block in a_all])

    inner_1 = jnp.stack([b[0][:1], b[2][:1], b[1][:1], b[3][:1]], axis=2)
    low_1 = depth_step(inner_1[0, 1], 1)
    high_1 = depth_step(inner_1[0, 0], -1)
    near_b = with_rows(b)

    far_reach = head_window[:, 0] == 1
    corner_reach = far_reach & (head_window[:, 1] == 1)
    rare = (jnp.sum(far_reach) > 2 * RING) | (jnp.sum(corner_reach) > RING)

    def full(near, low, high):
        low_c = depth_step(near[0, 1, 4:], 1)
        high_c = depth_step(near[0, 0, 4:], -1)
        low_2 = depth_step(near[1, 1], 1)
        high_2 = depth_step(near[1, 0], -1)
        return (
            jnp.stack([jnp.concatenate([low, low_c]), low_2]),
            jnp.stack([jnp.concatenate([high, high_c]), high_2]),
        )

    def common(near, low, high):
        pad = ((0, 4), (0, 0), (0, 0), (0, 0))
        filler = jnp.zeros((8, 2, TOK, DIM), jnp.bfloat16)
        return jnp.stack([jnp.pad(low, pad), filler]), jnp.stack([jnp.pad(high, pad), filler])

    low_b, high_b = lax.cond(rare, full, common, near_b, low_1, high_1)
    mine_b = [near_b.reshape(2, 16, 2, TOK, DIM), low_b, high_b]
    kv_b = jnp.concatenate(mine_b + [core_swap(block) for block in mine_b], axis=1)
    out_b = attend(light, head_window, valid_counts, kv_b, c)

    results = [jnp.concatenate([out_a[m], out_b[m]], axis=0) for m in range(RING)]
    return unpack(head_window, spread(results))


def solution(mesh):
    in_specs = (
        P("ta", "ha", "wa", None, None),
        P("ta", "ha", "wa", None, None),
        P("ta", "ha", "wa", None, None),
        P(),
        P(),
    )
    out_specs = P("ta", "ha", "wa", None, None)
    return jax.shard_map(
        on_device, mesh=mesh, in_specs=in_specs, out_specs=out_specs, check_vma=False
    )
```

```python
import functools

import jax
import jax.numpy as jnp
from jax import lax
from jax.experimental import pallas as pl
from jax.experimental.pallas import tpu as pltpu
from jax.sharding import PartitionSpec as P

HEADS = 12
DIM = 128
TOK = 192
NT, NH, NW = 8, 8, 4
RING = 4
SLOTS = HEADS // RING
CHUNK = 4
LOG2E = 1.4426950408889634
SCALE = DIM**-0.5 * LOG2E
PLANE = ("ha", "wa")
ANY = pl.BlockSpec(memory_space=pl.ANY)
HBM = pl.BlockSpec(memory_space=pltpu.HBM)
SMEM = pl.BlockSpec(memory_space=pltpu.SMEM)
VMEM = pl.BlockSpec(memory_space=pltpu.VMEM)


def plane_index(x, y, core):
    return (x * 2 + y % 2) * 4 + (y // 2) * 2 + core


PLANE_POS = [(x, y, core) for x in range(4) for y in range(4) for core in range(2)]


def ring_swap(block, mask):
    perm = [(plane_index(x, y, c), plane_index(x, y ^ mask, c)) for x, y, c in PLANE_POS]
    return lax.ppermute(block, PLANE, perm)


def core_swap(block):
    perm = [(plane_index(x, y, c), plane_index(x, y, 1 - c)) for x, y, c in PLANE_POS]
    return lax.ppermute(block, PLANE, perm)


def row_step(block, own):
    perm = []
    for x, y, c in PLANE_POS:
        target = x + 1 if (y % 2 == 1) == own else x - 1
        perm.append((plane_index(x, y, c), plane_index(target % 4, y, c)))
    return lax.ppermute(block, PLANE, perm)


def depth_step(block, step):
    return lax.ppermute(block, "ta", [(i, (i + step) % 4) for i in range(4)])


def place():
    plane_h = lax.axis_index("ha")
    plane_w = lax.axis_index("wa")
    return lax.axis_index("ta"), plane_h // 2, plane_h % 2, plane_w // 2, plane_w % 2


def rank_heads(window, order):
    keys, sizes = [], []
    for head in range(HEADS):
        t, h, w = (window[axis, head] for axis in range(3))
        keys.append((7 - (t * 4 + h * 2 + w)) * 16 + head)
        sizes.append((1 + 2 * t) * (1 + 2 * h) * (1 + 2 * w) * 16 + head)
    slots = []
    for head in range(HEADS):
        rank = jnp.int32(0)
        for other in range(HEADS):
            if other != head:
                rank += (keys[other] < keys[head]).astype(jnp.int32)
        slots.append(rank // RING)
    for head in range(HEADS):
        spot = jnp.int32(0)
        for other in range(HEADS):
            if other != head:
                ahead = (slots[other] == slots[head]) & (sizes[other] > sizes[head])
                spot += ahead.astype(jnp.int32)
        spot = jnp.where(slots[head] == 0, spot, RING - 1 - spot)
        order[slots[head] * RING + spot] = head


def pack_kernel(slots, window, keys, values, queries, *rest):
    order, sem = rest[-2:]
    rank_heads(window, order)
    _, _, y_lo, y_hi, _ = place()
    ring = y_hi * 2 + y_lo
    copies = []
    for n, slot in enumerate(slots):
        for mask in range(RING):
            head = order[slot * RING + (ring ^ mask)]
            cols = pl.ds(pl.multiple_of(head * DIM, DIM), DIM)
            for part, source in enumerate((keys, values, queries)):
                for t in range(2):
                    copies.append(
                        pltpu.make_async_copy(
                            source.at[t, 0, 0, :, cols], rest[n * RING + mask].at[t, part], sem
                        )
                    )
    for copy in copies:
        copy.start()
    for copy in copies:
        copy.wait()


def pack(slots, head_window, keys, values, queries):
    shape = jax.ShapeDtypeStruct((2, 3, TOK, DIM), jnp.bfloat16)
    outs = pl.pallas_call(
        functools.partial(pack_kernel, slots),
        out_shape=[shape] * (RING * len(slots)),
        in_specs=[SMEM] + [HBM] * 3,
        out_specs=[VMEM] * (RING * len(slots)),
        scratch_shapes=[pltpu.SMEM((HEADS,), jnp.int32), pltpu.SemaphoreType.DMA],
        compiler_params=pltpu.CompilerParams(vmem_limit_bytes=8 * 1024 * 1024),
        cost_estimate=pl.CostEstimate(flops=0, bytes_accessed=4_000_000, transcendentals=0),
    )(head_window, keys, values, queries)
    return [outs[n : n + RING] for n in range(0, len(outs), RING)]


def unpack_kernel(window, *rest):
    parts = rest[:RING]
    out, order, sem = rest[RING:]
    rank_heads(window, order)
    _, _, y_lo, y_hi, _ = place()
    ring = y_hi * 2 + y_lo
    copies = []
    for slot in range(SLOTS):
        for mask in range(RING):
            head = order[slot * RING + (ring ^ mask)]
            cols = pl.ds(pl.multiple_of(head * DIM, DIM), DIM)
            for t in range(2):
                copies.append(
                    pltpu.make_async_copy(
                        parts[mask].at[slot, t], out.at[t, 0, 0, :, cols], sem
                    )
                )
    for copy in copies:
        copy.start()
    for copy in copies:
        copy.wait()


def unpack(head_window, parts):
    return pl.pallas_call(
        unpack_kernel,
        out_shape=jax.ShapeDtypeStruct((2, 1, 1, TOK, HEADS * DIM), jnp.bfloat16),
        in_specs=[SMEM] + [ANY] * RING,
        out_specs=VMEM,
        scratch_shapes=[pltpu.SMEM((HEADS,), jnp.int32), pltpu.SemaphoreType.DMA],
        compiler_params=pltpu.CompilerParams(vmem_limit_bytes=4 * 1024 * 1024),
        cost_estimate=pl.CostEstimate(flops=0, bytes_accessed=2_400_000, transcendentals=0),
    )(head_window, *parts)


def list_tiles(counts, items, lives, chain, reach, glob, t, y_lo, y_hi, core, w):
    glob_t, glob_h = glob
    h = glob_h % 2

    def axis(position, extent, reach_here, code):
        out = []
        for step in (0, -1, 1):
            spot = position + step
            inside = (spot >= 0) & (spot < extent) & (abs(step) <= reach_here)
            out.append((inside.astype(jnp.int32), jnp.clip(spot, 0, extent - 1), code(step)))
        return out

    def code_t(step):
        return {0: 0, 1: 8, -1: 32, 2: 40}[t + step]

    def code_h(step):
        here = h + step
        row = jnp.where(here < 0, 1, jnp.where(here > 1, 0, here))
        halo = ((here < 0) | (here > 1)).astype(jnp.int32)
        return halo * 16 + (row ^ y_lo) * 2

    def code_w(step):
        here = jnp.clip(w + step, 0, NW - 1)
        return (here % 2 != core).astype(jnp.int32) * 4 + ((here // 2) ^ y_hi)

    over_t = axis(glob_t, NT, reach[0], code_t)
    over_h = axis(glob_h, NH, reach[1], code_h)
    over_w = axis(w, NW, reach[2], code_w)
    total = jnp.int32(0)
    for in_t, at_t, item_t in over_t:
        for in_h, at_h, item_h in over_h:
            for in_w, at_w, item_w in over_w:
                items[chain, total] = item_t + item_h + item_w
                lives[chain, total] = counts[at_t, at_w, at_h]
                total += in_t * in_h * in_w
    return total


CHAINS = 4


def attend_kernel(slots, window, counts, *rest):
    kvs, rest = rest[: len(slots)], rest[len(slots) :]
    q_in, rest = rest[: len(slots) * RING], rest[len(slots) * RING :]
    outs, rest = rest[:RING], rest[RING:]
    order, items, lives, q_mem, o_mem, *tables = rest
    rank_heads(window, order)
    z, x, y_lo, y_hi, core = place()
    for n, slot in enumerate(slots):
        kv = kvs[n]
        head = order[slot * RING + y_hi * 2 + y_lo]
        reach = [window[axis, head] for axis in range(3)]
        for mask in range(RING):
            for t in range(2):
                q_mem[mask * 2 + t] = q_in[n * RING + mask][t, 2]

        def column_pair(flip_hi, carry):
            w = 2 * (flip_hi ^ y_hi) + core
            totals, owns = [], []
            for chain in range(CHAINS):
                flip_lo, t = chain // 2, chain % 2
                glob = (2 * z + t, 2 * x + (flip_lo ^ y_lo))
                owns.append(counts[glob[0], w, glob[1]])
                totals.append(
                    list_tiles(
                        counts, items, lives, chain, reach, glob, t, y_lo, y_hi, core, w
                    )
                )
            most = functools.reduce(jnp.maximum, totals)
            chunks = (most + CHUNK - 1) // CHUNK
            for chain in range(CHAINS):

                def fill(spot, carry):
                    items[chain, spot] = items[chain, 0]
                    lives[chain, spot] = 0
                    return carry

                lax.fori_loop(totals[chain], (chunks + 1) * CHUNK, fill, 0)

            def score(chain, chunk):
                first = chunk * CHUNK
                spots = [items[chain, first + u] for u in range(CHUNK)]
                k_all = jnp.concatenate([kv[spot, 0] for spot in spots], axis=0)
                scores = lax.dot_general(
                    q_mem[flip_hi * 4 + chain], k_all, (((1,), (1,)), ((), ())),
                    preferred_element_type=jnp.float32,
                )
                column = lax.broadcasted_iota(jnp.int32, (1, CHUNK * TOK), 1)
                bias = jnp.full((1, CHUNK * TOK), -1e30, jnp.float32)
                for u in range(CHUNK):
                    edge = u * TOK
                    live = (column >= edge) & (column < edge + lives[chain, first + u])
                    bias = jnp.where(live, 0.0, bias)
                tables[chain][...] = scores * SCALE + bias

            def gather(chain, chunk, top, acc, den):
                first = chunk * CHUNK
                spots = [items[chain, first + u] for u in range(CHUNK)]
                v_all = jnp.concatenate([kv[spot, 1] for spot in spots], axis=0)
                scores = tables[chain][...]
                new_top = jnp.maximum(top, jnp.max(scores, axis=1, keepdims=True))
                weights = jnp.exp2(scores - new_top)
                gain = jnp.dot(
                    weights.astype(jnp.bfloat16), v_all, preferred_element_type=jnp.float32
                )
                part = functools.reduce(
                    jnp.add, [weights[:, c : c + DIM] for c in range(0, CHUNK * TOK, DIM)]
                )
                fade = jnp.exp2(top - new_top)
                return new_top, acc * fade + gain, den * fade + part

            score(0, 0)

            def one_chunk(chunk, state):
                after = []
                for chain in range(CHAINS):
                    if chain + 1 < CHAINS:
                        score(chain + 1, chunk)
                    else:
                        score(0, chunk + 1)
                    after.append(gather(chain, chunk, *state[chain]))
                return tuple(after)

            blank = (
                jnp.full((TOK, 1), -3e30, jnp.float32),
                jnp.zeros((TOK, DIM), jnp.float32),
                jnp.zeros((TOK, DIM), jnp.float32),
            )
            state = lax.fori_loop(0, chunks, one_chunk, (blank,) * CHAINS)
            row = lax.broadcasted_iota(jnp.int32, (TOK, DIM), 0)
            for chain in range(CHAINS):
                _, acc, den = state[chain]
                result = acc / jnp.sum(den, axis=1, keepdims=True)
                result = jnp.where(row < owns[chain], result, 0.0).astype(jnp.bfloat16)
                o_mem[flip_hi * 4 + chain] = result
            return carry

        lax.fori_loop(0, 2, column_pair, 0)
        for mask in range(RING):
            for t in range(2):
                outs[mask][n, t] = o_mem[mask * 2 + t]


def attend(slots, head_window, valid_counts, kvs, q_parts, work):
    shape = jax.ShapeDtypeStruct((len(slots), 2, TOK, DIM), jnp.bfloat16)
    return pl.pallas_call(
        functools.partial(attend_kernel, slots),
        out_shape=[shape] * RING,
        in_specs=[SMEM, SMEM] + [VMEM] * (len(slots) + len(slots) * RING),
        out_specs=[VMEM] * RING,
        scratch_shapes=[
            pltpu.SMEM((HEADS,), jnp.int32),
            pltpu.SMEM((CHAINS, 27 + 2 * CHUNK), jnp.int32),
            pltpu.SMEM((CHAINS, 27 + 2 * CHUNK), jnp.int32),
            pltpu.VMEM((2 * RING, TOK, DIM), jnp.bfloat16),
            pltpu.VMEM((2 * RING, TOK, DIM), jnp.bfloat16),
        ]
        + [pltpu.VMEM((TOK, CHUNK * TOK), jnp.float32)] * CHAINS,
        compiler_params=pltpu.CompilerParams(vmem_limit_bytes=12 * 1024 * 1024),
        cost_estimate=pl.CostEstimate(
            flops=work, bytes_accessed=len(slots) * 6_500_000, transcendentals=5_000_000
        ),
    )(head_window, valid_counts, *kvs, *q_parts)


def spread(parts):
    return [parts[0]] + [ring_swap(parts[mask], mask) for mask in range(1, RING)]


def row_tiles(*slots):
    own = [jnp.stack([a[0][:, :2], a[2][:, :2]], axis=1) for a in slots]
    other = [jnp.stack([a[1][:, :2], a[3][:, :2]], axis=1) for a in slots]
    return row_step(jnp.stack(own), True), row_step(jnp.stack(other), False)


def near_tiles(a, rows, n):
    inner = jnp.stack([a[m][:, :2] for m in (0, 2, 1, 3)], axis=1)
    return jnp.concatenate([inner, rows[0][n], rows[1][n]], axis=1)


def depth_tiles(block):
    return depth_step(block[1], 1), depth_step(block[0], -1)


def gather_tiles(near, near_other, *far):
    pieces = []
    for part in (slice(0, 4), slice(4, 8)):
        for t in range(2):
            pieces += [near[t, part], near_other[t, part]]
    for block, block_other in far:
        for t in range(2):
            pieces += [block[t], block_other[t]]
    return jnp.concatenate(pieces, axis=0)


def halves(block, block_other):
    return [(block[:, :4], block_other[:, :4]), (block[:, 4:], block_other[:, 4:])]


def pipeline(full, head_window, valid_counts, keys, values, queries):
    (a0,) = pack((0,), head_window, keys, values, queries)
    a1, a2 = pack((1, 2), head_window, keys, values, queries)

    a0 = spread(a0)
    a0, a1 = lax.optimization_barrier((a0, a1))

    rows_0 = row_tiles(a0)
    a1 = spread(a1)
    a0, rows_0, a1, a2 = lax.optimization_barrier((a0, rows_0, a1, a2))

    near_0 = near_tiles(a0, rows_0, 0)
    far_0 = depth_tiles(near_0)
    a2 = spread(a2)
    near_0, far_0, a1, a2 = lax.optimization_barrier((near_0, far_0, a1, a2))
    near_0_other = core_swap(near_0)

    far_0 = jnp.stack(far_0)
    inner_1 = jnp.stack([a1[m][:, :2] for m in (0, 2, 1, 3)], axis=1)
    ends_1 = depth_tiles(inner_1)
    rows_12 = row_tiles(a1, a2)
    tiles = gather_tiles(near_0, near_0_other, *halves(far_0, core_swap(far_0)))
    out_a = attend((0,), head_window, valid_counts, [tiles], a0, 20_000_000_000)
    out_a, ends_1, rows_12 = lax.optimization_barrier((out_a, ends_1, rows_12))

    ends_1 = jnp.stack(ends_1)
    near_1, near_2 = near_tiles(a1, rows_12, 0), near_tiles(a2, rows_12, 1)
    far_1 = [(ends_1, core_swap(ends_1))]
    far_2 = []
    if full:
        corners = jnp.stack(depth_tiles(near_1[:, 4:]))
        last = jnp.stack(depth_tiles(near_2))
        far_1.append((corners, core_swap(corners)))
        far_2 = halves(last, core_swap(last))
    tiles = [
        gather_tiles(near_1, core_swap(near_1), *far_1),
        gather_tiles(near_2, core_swap(near_2), *far_2),
    ]
    out_b = attend((1, 2), head_window, valid_counts, tiles, [*a1, *a2], 20_000_000_000)
    return spread([jnp.concatenate([out_a[m], out_b[m]], axis=0) for m in range(RING)])


def on_device(queries, keys, values, valid_counts, head_window):
    far_reach = head_window[:, 0] == 1
    corner_reach = far_reach & (head_window[:, 1] == 1)
    rare = (jnp.sum(far_reach) > 2 * RING) | (jnp.sum(corner_reach) > RING)
    window = head_window.T
    results = lax.cond(
        jnp.logical_not(rare),
        functools.partial(pipeline, False),
        functools.partial(pipeline, True),
        window, valid_counts.transpose(0, 2, 1), keys, values, queries,
    )
    return unpack(window, results)


def solution(mesh):
    in_specs = (
        P("ta", "ha", "wa", None, None),
        P("ta", "ha", "wa", None, None),
        P("ta", "ha", "wa", None, None),
        P(),
        P(),
    )
    out_specs = P("ta", "ha", "wa", None, None)
    return jax.shard_map(
        on_device, mesh=mesh, in_specs=in_specs, out_specs=out_specs, check_vma=False
    )
```

```python
import functools

import jax
import jax.numpy as jnp
from jax import lax
from jax.experimental import pallas as pl
from jax.experimental.pallas import tpu as pltpu
from jax.sharding import PartitionSpec as P

HEADS = 12
DIM = 128
TOK = 192
NT, NH, NW = 8, 8, 4
RING = 4
SLOTS = HEADS // RING
CHUNK = 6
LOG2E = 1.4426950408889634
SCALE = DIM**-0.5 * LOG2E
PLANE = ("ha", "wa")
ANY = pl.BlockSpec(memory_space=pl.ANY)
HBM = pl.BlockSpec(memory_space=pltpu.HBM)
SMEM = pl.BlockSpec(memory_space=pltpu.SMEM)
VMEM = pl.BlockSpec(memory_space=pltpu.VMEM)


def plane_index(x, y, core):
    return (x * 2 + y % 2) * 4 + (y // 2) * 2 + core


PLANE_POS = [(x, y, core) for x in range(4) for y in range(4) for core in range(2)]


def ring_swap(block, mask):
    perm = [(plane_index(x, y, c), plane_index(x, y ^ mask, c)) for x, y, c in PLANE_POS]
    return lax.ppermute(block, PLANE, perm)


def core_swap(block):
    perm = [(plane_index(x, y, c), plane_index(x, y, 1 - c)) for x, y, c in PLANE_POS]
    return lax.ppermute(block, PLANE, perm)


def row_step(block, own):
    perm = []
    for x, y, c in PLANE_POS:
        target = x + 1 if (y % 2 == 1) == own else x - 1
        perm.append((plane_index(x, y, c), plane_index(target % 4, y, c)))
    return lax.ppermute(block, PLANE, perm)


def depth_step(block, step):
    return lax.ppermute(block, "ta", [(i, (i + step) % 4) for i in range(4)])


def place():
    plane_h = lax.axis_index("ha")
    plane_w = lax.axis_index("wa")
    return lax.axis_index("ta"), plane_h // 2, plane_h % 2, plane_w // 2, plane_w % 2


def rank_heads(window, order):
    keys, sizes = [], []
    for head in range(HEADS):
        t, h, w = (window[axis, head] for axis in range(3))
        keys.append((7 - (t * 4 + h * 2 + w)) * 16 + head)
        sizes.append((1 + 2 * t) * (1 + 2 * h) * (1 + 2 * w) * 16 + head)
    slots = []
    for head in range(HEADS):
        rank = jnp.int32(0)
        for other in range(HEADS):
            if other != head:
                rank += (keys[other] < keys[head]).astype(jnp.int32)
        slots.append(rank // RING)
    for head in range(HEADS):
        spot = jnp.int32(0)
        for other in range(HEADS):
            if other != head:
                ahead = (slots[other] == slots[head]) & (sizes[other] > sizes[head])
                spot += ahead.astype(jnp.int32)
        spot = jnp.where(slots[head] == 0, spot, RING - 1 - spot)
        order[slots[head] * RING + spot] = head


def pack_kernel(slots, window, keys, values, queries, *rest):
    order, sem = rest[-2:]
    rank_heads(window, order)
    _, _, y_lo, y_hi, _ = place()
    ring = y_hi * 2 + y_lo
    copies = []
    for n, slot in enumerate(slots):
        for mask in range(RING):
            head = order[slot * RING + (ring ^ mask)]
            cols = pl.ds(pl.multiple_of(head * DIM, DIM), DIM)
            for part, source in enumerate((keys, values, queries)):
                for t in range(2):
                    copies.append(
                        pltpu.make_async_copy(
                            source.at[t, 0, 0, :, cols], rest[n * RING + mask].at[t, part], sem
                        )
                    )
    for copy in copies:
        copy.start()
    for copy in copies:
        copy.wait()


def pack(slots, head_window, keys, values, queries):
    shape = jax.ShapeDtypeStruct((2, 3, TOK, DIM), jnp.bfloat16)
    outs = pl.pallas_call(
        functools.partial(pack_kernel, slots),
        out_shape=[shape] * (RING * len(slots)),
        in_specs=[SMEM] + [HBM] * 3,
        out_specs=[VMEM] * (RING * len(slots)),
        scratch_shapes=[pltpu.SMEM((HEADS,), jnp.int32), pltpu.SemaphoreType.DMA],
        compiler_params=pltpu.CompilerParams(vmem_limit_bytes=8 * 1024 * 1024),
        cost_estimate=pl.CostEstimate(flops=0, bytes_accessed=4_000_000, transcendentals=0),
    )(head_window, keys, values, queries)
    return [outs[n : n + RING] for n in range(0, len(outs), RING)]


def unpack_kernel(window, *rest):
    parts = rest[:RING]
    out, order, sem = rest[RING:]
    rank_heads(window, order)
    _, _, y_lo, y_hi, _ = place()
    ring = y_hi * 2 + y_lo
    copies = []
    for slot in range(SLOTS):
        for mask in range(RING):
            head = order[slot * RING + (ring ^ mask)]
            cols = pl.ds(pl.multiple_of(head * DIM, DIM), DIM)
            for t in range(2):
                copies.append(
                    pltpu.make_async_copy(
                        parts[mask].at[slot, t], out.at[t, 0, 0, :, cols], sem
                    )
                )
    for copy in copies:
        copy.start()
    for copy in copies:
        copy.wait()


def unpack(head_window, parts):
    return pl.pallas_call(
        unpack_kernel,
        out_shape=jax.ShapeDtypeStruct((2, 1, 1, TOK, HEADS * DIM), jnp.bfloat16),
        in_specs=[SMEM] + [ANY] * RING,
        out_specs=VMEM,
        scratch_shapes=[pltpu.SMEM((HEADS,), jnp.int32), pltpu.SemaphoreType.DMA],
        compiler_params=pltpu.CompilerParams(vmem_limit_bytes=4 * 1024 * 1024),
        cost_estimate=pl.CostEstimate(flops=0, bytes_accessed=2_400_000, transcendentals=0),
    )(head_window, *parts)


def list_tiles(counts, items, lives, chain, reach, glob, t, y_lo, y_hi, core, w):
    glob_t, glob_h = glob
    h = glob_h % 2

    def axis(position, extent, reach_here, code):
        out = []
        for step in (0, -1, 1):
            spot = position + step
            inside = (spot >= 0) & (spot < extent) & (abs(step) <= reach_here)
            out.append((inside.astype(jnp.int32), jnp.clip(spot, 0, extent - 1), code(step)))
        return out

    def code_t(step):
        return {0: 0, 1: 8, -1: 32, 2: 40}[t + step]

    def code_h(step):
        here = h + step
        row = jnp.where(here < 0, 1, jnp.where(here > 1, 0, here))
        halo = ((here < 0) | (here > 1)).astype(jnp.int32)
        return halo * 16 + (row ^ y_lo) * 2

    def code_w(step):
        here = jnp.clip(w + step, 0, NW - 1)
        return (here % 2 != core).astype(jnp.int32) * 4 + ((here // 2) ^ y_hi)

    over_t = axis(glob_t, NT, reach[0], code_t)
    over_h = axis(glob_h, NH, reach[1], code_h)
    over_w = axis(w, NW, reach[2], code_w)
    total = jnp.int32(0)
    for in_t, at_t, item_t in over_t:
        for in_h, at_h, item_h in over_h:
            for in_w, at_w, item_w in over_w:
                items[chain, total] = item_t + item_h + item_w
                lives[chain, total] = counts[at_t, at_w, at_h]
                total += in_t * in_h * in_w
    return total


CHAINS = 4


def attend_kernel(slots, window, counts, *rest):
    kvs, rest = rest[: len(slots)], rest[len(slots) :]
    q_in, rest = rest[: len(slots) * RING], rest[len(slots) * RING :]
    outs, rest = rest[:RING], rest[RING:]
    order, items, lives, q_mem, o_mem, *tables = rest
    rank_heads(window, order)
    z, x, y_lo, y_hi, core = place()
    for n, slot in enumerate(slots):
        kv = kvs[n]
        head = order[slot * RING + y_hi * 2 + y_lo]
        reach = [window[axis, head] for axis in range(3)]
        for mask in range(RING):
            for t in range(2):
                q_mem[mask * 2 + t] = q_in[n * RING + mask][t, 2]

        def column_pair(flip_hi, carry):
            w = 2 * (flip_hi ^ y_hi) + core
            totals, owns = [], []
            for chain in range(CHAINS):
                flip_lo, t = chain // 2, chain % 2
                glob = (2 * z + t, 2 * x + (flip_lo ^ y_lo))
                owns.append(counts[glob[0], w, glob[1]])
                totals.append(
                    list_tiles(
                        counts, items, lives, chain, reach, glob, t, y_lo, y_hi, core, w
                    )
                )
            most = functools.reduce(jnp.maximum, totals)
            chunks = (most + CHUNK - 1) // CHUNK
            for chain in range(CHAINS):

                def fill(spot, carry):
                    items[chain, spot] = items[chain, 0]
                    lives[chain, spot] = 0
                    return carry

                lax.fori_loop(totals[chain], (chunks + 1) * CHUNK, fill, 0)

            def score(chain, chunk):
                first = chunk * CHUNK
                spots = [items[chain, first + u] for u in range(CHUNK)]
                k_all = jnp.concatenate([kv[spot, 0] for spot in spots], axis=0)
                scores = lax.dot_general(
                    q_mem[flip_hi * 4 + chain], k_all, (((1,), (1,)), ((), ())),
                    preferred_element_type=jnp.float32,
                )
                column = lax.broadcasted_iota(jnp.int32, (1, CHUNK * TOK), 1)
                bias = jnp.full((1, CHUNK * TOK), -1e30, jnp.float32)
                for u in range(CHUNK):
                    edge = u * TOK
                    live = (column >= edge) & (column < edge + lives[chain, first + u])
                    bias = jnp.where(live, 0.0, bias)
                tables[chain][...] = scores * SCALE + bias

            def gather(chain, chunk, top, acc, den):
                first = chunk * CHUNK
                spots = [items[chain, first + u] for u in range(CHUNK)]
                v_all = jnp.concatenate([kv[spot, 1] for spot in spots], axis=0)
                scores = tables[chain][...]
                new_top = jnp.maximum(top, jnp.max(scores, axis=1, keepdims=True))
                weights = jnp.exp2(scores - new_top)
                gain = jnp.dot(
                    weights.astype(jnp.bfloat16), v_all, preferred_element_type=jnp.float32
                )
                part = functools.reduce(
                    jnp.add, [weights[:, c : c + DIM] for c in range(0, CHUNK * TOK, DIM)]
                )
                fade = jnp.exp2(top - new_top)
                return new_top, acc * fade + gain, den * fade + part

            score(0, 0)

            def one_chunk(chunk, state):
                after = []
                for chain in range(CHAINS):
                    if chain + 1 < CHAINS:
                        score(chain + 1, chunk)
                    else:
                        score(0, chunk + 1)
                    after.append(gather(chain, chunk, *state[chain]))
                return tuple(after)

            blank = (
                jnp.full((TOK, 1), -3e30, jnp.float32),
                jnp.zeros((TOK, DIM), jnp.float32),
                jnp.zeros((TOK, DIM), jnp.float32),
            )
            state = lax.fori_loop(0, chunks, one_chunk, (blank,) * CHAINS)
            row = lax.broadcasted_iota(jnp.int32, (TOK, DIM), 0)
            for chain in range(CHAINS):
                _, acc, den = state[chain]
                result = acc / jnp.sum(den, axis=1, keepdims=True)
                result = jnp.where(row < owns[chain], result, 0.0).astype(jnp.bfloat16)
                o_mem[flip_hi * 4 + chain] = result
            return carry

        lax.fori_loop(0, 2, column_pair, 0)
        for mask in range(RING):
            for t in range(2):
                outs[mask][n, t] = o_mem[mask * 2 + t]


def attend(slots, head_window, valid_counts, kvs, q_parts, work):
    shape = jax.ShapeDtypeStruct((len(slots), 2, TOK, DIM), jnp.bfloat16)
    return pl.pallas_call(
        functools.partial(attend_kernel, slots),
        out_shape=[shape] * RING,
        in_specs=[SMEM, SMEM] + [VMEM] * (len(slots) + len(slots) * RING),
        out_specs=[VMEM] * RING,
        scratch_shapes=[
            pltpu.SMEM((HEADS,), jnp.int32),
            pltpu.SMEM((CHAINS, 27 + 2 * CHUNK), jnp.int32),
            pltpu.SMEM((CHAINS, 27 + 2 * CHUNK), jnp.int32),
            pltpu.VMEM((2 * RING, TOK, DIM), jnp.bfloat16),
            pltpu.VMEM((2 * RING, TOK, DIM), jnp.bfloat16),
        ]
        + [pltpu.VMEM((TOK, CHUNK * TOK), jnp.float32)] * CHAINS,
        compiler_params=pltpu.CompilerParams(vmem_limit_bytes=12 * 1024 * 1024),
        cost_estimate=pl.CostEstimate(
            flops=work, bytes_accessed=len(slots) * 6_500_000, transcendentals=5_000_000
        ),
    )(head_window, valid_counts, *kvs, *q_parts)


def spread(parts):
    return [parts[0]] + [ring_swap(parts[mask], mask) for mask in range(1, RING)]


def row_tiles(*slots):
    own = [jnp.stack([a[0][:, :2], a[2][:, :2]], axis=1) for a in slots]
    other = [jnp.stack([a[1][:, :2], a[3][:, :2]], axis=1) for a in slots]
    return row_step(jnp.stack(own), True), row_step(jnp.stack(other), False)


def near_tiles(a, rows, n):
    inner = jnp.stack([a[m][:, :2] for m in (0, 2, 1, 3)], axis=1)
    return jnp.concatenate([inner, rows[0][n], rows[1][n]], axis=1)


def depth_tiles(block):
    return depth_step(block[1], 1), depth_step(block[0], -1)


def gather_tiles(near, near_other, *far):
    pieces = []
    for part in (slice(0, 4), slice(4, 8)):
        for t in range(2):
            pieces += [near[t, part], near_other[t, part]]
    for block, block_other in far:
        for t in range(2):
            pieces += [block[t], block_other[t]]
    return jnp.concatenate(pieces, axis=0)


def halves(block, block_other):
    return [(block[:, :4], block_other[:, :4]), (block[:, 4:], block_other[:, 4:])]


def pipeline(full, head_window, valid_counts, keys, values, queries):
    (a0,) = pack((0,), head_window, keys, values, queries)
    a1, a2 = pack((1, 2), head_window, keys, values, queries)

    a0 = spread(a0)
    a0, a1 = lax.optimization_barrier((a0, a1))

    rows_0 = row_tiles(a0)
    a1 = spread(a1)
    a0, rows_0, a1, a2 = lax.optimization_barrier((a0, rows_0, a1, a2))

    near_0 = near_tiles(a0, rows_0, 0)
    far_0 = depth_tiles(near_0)
    a2 = spread(a2)
    near_0, far_0, a1, a2 = lax.optimization_barrier((near_0, far_0, a1, a2))
    near_0_other = core_swap(near_0)

    far_0 = jnp.stack(far_0)
    inner_1 = jnp.stack([a1[m][:, :2] for m in (0, 2, 1, 3)], axis=1)
    ends_1 = depth_tiles(inner_1)
    rows_12 = row_tiles(a1, a2)
    tiles = gather_tiles(near_0, near_0_other, *halves(far_0, core_swap(far_0)))
    out_a = attend((0,), head_window, valid_counts, [tiles], a0, 20_000_000_000)
    out_a, ends_1, rows_12 = lax.optimization_barrier((out_a, ends_1, rows_12))

    ends_1 = jnp.stack(ends_1)
    near_1, near_2 = near_tiles(a1, rows_12, 0), near_tiles(a2, rows_12, 1)
    far_1 = [(ends_1, core_swap(ends_1))]
    far_2 = []
    if full:
        corners = jnp.stack(depth_tiles(near_1[:, 4:]))
        last = jnp.stack(depth_tiles(near_2))
        far_1.append((corners, core_swap(corners)))
        far_2 = halves(last, core_swap(last))
    tiles = [
        gather_tiles(near_1, core_swap(near_1), *far_1),
        gather_tiles(near_2, core_swap(near_2), *far_2),
    ]
    out_b = attend((1, 2), head_window, valid_counts, tiles, [*a1, *a2], 20_000_000_000)
    return spread([jnp.concatenate([out_a[m], out_b[m]], axis=0) for m in range(RING)])


def on_device(queries, keys, values, valid_counts, head_window):
    far_reach = head_window[:, 0] == 1
    corner_reach = far_reach & (head_window[:, 1] == 1)
    rare = (jnp.sum(far_reach) > 2 * RING) | (jnp.sum(corner_reach) > RING)
    window = head_window.T
    results = lax.cond(
        jnp.logical_not(rare),
        functools.partial(pipeline, False),
        functools.partial(pipeline, True),
        window, valid_counts.transpose(0, 2, 1), keys, values, queries,
    )
    return unpack(window, results)


def solution(mesh):
    in_specs = (
        P("ta", "ha", "wa", None, None),
        P("ta", "ha", "wa", None, None),
        P("ta", "ha", "wa", None, None),
        P(),
        P(),
    )
    out_specs = P("ta", "ha", "wa", None, None)
    return jax.shard_map(
        on_device, mesh=mesh, in_specs=in_specs, out_specs=out_specs, check_vma=False
    )
```
